32 devices in a mesh: dp: 4 (over y, core), context: 8 (over z, x).
Axes of the slice: x: 2, y: 2, z: 4, core: 2. Of those that a mesh axis runs over, the one named last changes fastest.
Arguments:
- queries: bfloat16 [4, 1024, 2048], P('dp', 'context'), may hold values from -6 to 6
- keys: bfloat16 [4, 1024, 2048], P('dp', 'context'), may hold values from -6 to 6
- values: bfloat16 [4, 1024, 2048], P('dp', 'context'), may hold values from -6 to 6
- out_grad: bfloat16 [4, 1024, 2048], P('dp', 'context'), may hold values from -6 to 6
- log_gates: float32 [4, 16, 1024], P('dp', None, 'context'), may hold values from -1 to 0, as said below
- query_map: bfloat16 [16, 128, 128], replicated, may hold values from -0.5 to 0.5
- key_map: bfloat16 [16, 128, 128], replicated, may hold values from -0.5 to 0.5
Outputs:
- query_grad: bfloat16 [4, 1024, 2048], P('dp', 'context')
- key_grad: bfloat16 [4, 1024, 2048], P('dp', 'context')
- value_grad: bfloat16 [4, 1024, 2048], P('dp', 'context')
- map_grads: float32 [4096, 128], P(('dp', 'context'))
The draws below stay inside these ranges and needn't reach their ends.
Inputs may be any that keep to these rules, and one draw needn't show every extreme that they name: `log_gates`: every entry is negative.
All inputs are finite; a program needn't handle non-finite values.
Results may differ from the reference program's by a relative error of at most 0.019.
Values may be sent and summed in bfloat16 or wider, within the bound.
A program may use at most 128 MiB of HBM per device.

```python
import math
import jax
import jax.numpy as jnp
from jax import lax

LOCAL_HEADS = 16
DH = 128
TOK_DEV = 128
BATCH_SEQUENCES = 4
SEQUENCE_LENGTH = 1024
TOKENS = 4096


def draw_log_gates(key, part):
    gathered_keys = jax.random.split(key, 7)
    picker = jax.random.uniform(gathered_keys[0], (BATCH_SEQUENCES, LOCAL_HEADS, 1))
    fast = picker < 0.5
    fast_rate = math.log(10.0) / jnp.exp(jax.random.uniform(gathered_keys[1], (BATCH_SEQUENCES, LOCAL_HEADS, 1), minval=math.log(30.0), maxval=math.log(50.0)))
    slow_rate = 0.15 * math.log(10.0) / SEQUENCE_LENGTH * jax.random.uniform(gathered_keys[2], (BATCH_SEQUENCES, LOCAL_HEADS, 1), minval=0.5, maxval=1.0)
    rate = jnp.where(fast, fast_rate, slow_rate)
    block_factor = jnp.exp(jax.random.uniform(gathered_keys[3], (BATCH_SEQUENCES, LOCAL_HEADS, SEQUENCE_LENGTH // TOK_DEV), minval=-0.7, maxval=0.7))
    factor = jnp.repeat(block_factor, TOK_DEV, axis=2)
    jitter = jax.random.uniform(gathered_keys[4], (BATCH_SEQUENCES, LOCAL_HEADS, SEQUENCE_LENGTH), minval=0.5, maxval=1.5)
    drawn_gates = -rate * factor * jitter
    token_spots = jax.random.randint(gathered_keys[5], (BATCH_SEQUENCES, LOCAL_HEADS, 2), 0, SEQUENCE_LENGTH)
    token_place = jnp.arange(SEQUENCE_LENGTH)[None, None, :]
    spike_mask = (token_place == token_spots[:, :, 0:1]) | (token_place == token_spots[:, :, 1:2])
    spike_gates = jnp.log(jax.random.uniform(gathered_keys[6], (BATCH_SEQUENCES, LOCAL_HEADS, SEQUENCE_LENGTH), minval=0.5, maxval=0.8))
    return (drawn_gates + jnp.where(spike_mask, spike_gates, 0.0)).astype(jnp.float32)


def shard_levels(own_key, shape, pieces, least, high):
    def one(dim, parts):
        draws = jax.random.uniform(jax.random.fold_in(jax.random.fold_in(own_key, 6), dim), (parts,), jnp.float32, least / len(pieces), high / len(pieces))
        return jnp.repeat(jnp.exp(draws), shape[dim] // parts).reshape((-1,) + (1,) * (len(shape) - dim - 1))

    gain = one(*pieces[0])
    for cut in pieces[1:]:
        gain = gain * one(*cut)
    return gain


def centred(stream_key, extent, width, reach, shards=(), kind=jnp.bfloat16):
    values = width * jax.random.normal(stream_key, extent, jnp.float32)
    if shards:
        values = values * shard_levels(stream_key, extent, shards, -0.22, 0.18)
    return jnp.clip(values, -reach, reach).astype(kind)


def setup_inputs(seed: int = 0) -> dict:
    key_list = jax.random.split(jax.random.key(seed), 8)
    queries = centred(key_list[0], (BATCH_SEQUENCES, SEQUENCE_LENGTH, LOCAL_HEADS * DH), 1.0, 6.0, ((0, 4), (1, 8)))
    keys = centred(key_list[1], (BATCH_SEQUENCES, SEQUENCE_LENGTH, LOCAL_HEADS * DH), 1.0, 6.0, ((0, 4), (1, 8)))
    values = centred(key_list[2], (BATCH_SEQUENCES, SEQUENCE_LENGTH, LOCAL_HEADS * DH), 1.0, 6.0, ((0, 4), (1, 8)))
    out_grad = centred(key_list[3], (BATCH_SEQUENCES, SEQUENCE_LENGTH, LOCAL_HEADS * DH), 1.0, 6.0, ((0, 4), (1, 8)))
    log_gates = draw_log_gates(jax.random.fold_in(key_list[7], 71), 0)
    query_map = centred(key_list[5], (LOCAL_HEADS, DH, DH), DH ** -0.5, 0.5)
    key_map = centred(key_list[6], (LOCAL_HEADS, DH, DH), DH ** -0.5, 0.5)
    return dict(queries=queries, keys=keys, values=values, out_grad=out_grad, log_gates=log_gates, query_map=query_map, key_map=key_map)


exact_mode = lax.Precision.HIGHEST


def rounded(array):
    return lax.optimization_barrier(array.astype(jnp.bfloat16)).astype(jnp.float32)


def decay_tables(gates):
    running = jnp.cumsum(gates, axis=2)
    closing = running[:, :, -1]
    length = gates.shape[2]
    causal = jnp.arange(length)[:, None] >= jnp.arange(length)[None, :]
    spread = running[:, :, :, None] - running[:, :, None, :]
    within = jnp.where(causal, jnp.exp(jnp.where(causal, spread, 0.0)), 0.0)
    to_end = jnp.exp(closing[:, :, None] - running)
    from_start = jnp.exp(running)
    return within, to_end, from_start, jnp.exp(rounded(closing))


def reference(queries, keys, values, out_grad, log_gates, query_map, key_map):
    spans = SEQUENCE_LENGTH // TOK_DEV
    key_scale = DH ** -0.5 / 16.0
    map_query = query_map.astype(jnp.float32)
    map_key = key_map.astype(jnp.float32)

    def one_sequence(items):
        query_seq, key_seq, value_seq, grad_seq, gate_seq = items
        shape = (spans, TOK_DEV, LOCAL_HEADS, DH)
        query_heads = query_seq.reshape(shape).astype(jnp.float32)
        key_heads = key_seq.reshape(shape).astype(jnp.float32)
        value_heads = value_seq.reshape(shape).astype(jnp.float32)
        grad_heads = grad_seq.reshape(shape).astype(jnp.float32)
        gates = gate_seq.reshape(LOCAL_HEADS, spans, TOK_DEV).transpose(1, 0, 2)
        query_feat = rounded(jnp.einsum("btha,had->bthd", query_heads, map_query))
        key_feat = rounded(jnp.einsum("btha,had->bthd", key_heads, map_key) * key_scale)
        within, to_end, from_start, decay = decay_tables(gates)
        scores = rounded(jnp.einsum("bthd,bshd->bhts", query_feat, key_feat) * within)
        grad_scores = rounded(jnp.einsum("bthd,bshd->bhts", grad_heads, value_heads) * within)
        states_local = rounded(jnp.einsum("bshi,bhs,bshj->bhij", key_feat, to_end, value_heads, precision=exact_mode))
        grads_local = rounded(jnp.einsum("bthi,bht,bthj->bhij", query_feat, from_start, grad_heads, precision=exact_mode))

        def carry_on(carry, item):
            factor, block = item
            return factor[:, None, None] * carry + block, carry

        anchor = jnp.zeros((LOCAL_HEADS, DH, DH), jnp.float32)
        _, state_in = lax.scan(carry_on, anchor, (decay, states_local))
        _, grad_in = lax.scan(carry_on, anchor, (decay, grads_local), reverse=True)
        state_in = rounded(state_in)
        grad_in = rounded(grad_in)
        start_weight = jnp.transpose(from_start, (0, 2, 1))[..., None]
        end_weight = jnp.transpose(to_end, (0, 2, 1))[..., None]
        query_total = jnp.einsum("bhts,bshd->bthd", grad_scores, key_feat) + jnp.einsum("bthj,bhij->bthi", grad_heads, state_in, precision=exact_mode) * start_weight
        key_total = jnp.einsum("bhts,bthd->bshd", grad_scores, query_feat) + jnp.einsum("bshj,bhij->bshi", value_heads, grad_in, precision=exact_mode) * end_weight
        value_total = jnp.einsum("bhts,bthd->bshd", scores, grad_heads) + jnp.einsum("bshi,bhij->bshj", key_feat, grad_in, precision=exact_mode) * end_weight
        query_back = rounded(query_total)
        key_back = rounded(key_total * key_scale)
        query_out = jnp.einsum("bthd,had->btha", query_back, map_query).astype(jnp.bfloat16).reshape(SEQUENCE_LENGTH, LOCAL_HEADS * DH)
        key_out = jnp.einsum("bthd,had->btha", key_back, map_key).astype(jnp.bfloat16).reshape(SEQUENCE_LENGTH, LOCAL_HEADS * DH)
        value_out = value_total.astype(jnp.bfloat16).reshape(SEQUENCE_LENGTH, LOCAL_HEADS * DH)
        map_part = jnp.stack([jnp.einsum("btha,bthd->had", query_heads, query_back), jnp.einsum("btha,bthd->had", key_heads, key_back)])
        return query_out, key_out, value_out, map_part

    results = lax.map(one_sequence, (queries, keys, values, out_grad, log_gates))
    map_grads = (jnp.sum(results[3], axis=0) * (TOKENS ** -0.5)).reshape(2 * LOCAL_HEADS * DH, DH)
    return results[0], results[1], results[2], map_grads
```

```python
import functools

import jax
import jax.numpy as jnp
from jax import lax
from jax.experimental import pallas as pl
from jax.experimental.pallas import tpu as pltpu
from jax.sharding import PartitionSpec as P

MESH = pl.DeviceIdType.MESH
BF16, F32 = jnp.bfloat16, jnp.float32


def nn(a, b):
    return lax.dot_general(a, b, (((1,), (0,)), ((), ())), preferred_element_type=F32)


def nt(a, b):
    return lax.dot_general(a, b, (((1,), (1,)), ((), ())), preferred_element_type=F32)


def tn(a, b):
    return lax.dot_general(a, b, (((0,), (0,)), ((), ())), preferred_element_type=F32)


def kernel(
    sizes, q_ref, k_ref, v_ref, o_ref, gate_ref, wq_ref, wk_ref,
    dq_ref, dk_ref, dv_ref, dm_ref,
    run, fq, fk, qt, kt, vt, xg, cl, zin, zout, pm, rc, sy, ry, a2, sz, rz, a3, sx, rx,
    c_send, c_recv, x_send, x_recv, z_send, z_recv,
    rc_send, rc_recv, ry_send, ry_recv, rz_send, rz_recv, rx_send, rx_recv,
):
    Y, Z, X, H, W, T, NG, HP, map_scale = sizes
    key_scale = W ** (-0.5) / 16.0
    dp, ctx = lax.axis_index("dp"), lax.axis_index("context")
    y, core = lax.div(dp, 2), lax.rem(dp, 2)
    z, x = lax.div(ctx, X), lax.rem(ctx, X)
    x_peer = lambda i: (dp, z * X + lax.rem(x + i, X))
    z_peer = lambda i: (dp, lax.rem(z + i, Z) * X + x)
    y_peer = lambda i: (lax.rem(y + i, Y) * 2 + core, ctx)
    core_peer = (y * 2 + 1 - core, ctx)

    peers = [x_peer(i) for i in range(1, X)] + [z_peer(i) for i in range(1, Z)]
    peers += [y_peer(i) for i in range(1, Y)] + [core_peer]
    barrier = pltpu.get_barrier_semaphore()
    for peer in peers:
        pl.semaphore_signal(barrier, inc=1, device_id=peer, device_id_type=MESH)

    def remote(src, dst, send, recv, peer):
        return pltpu.make_async_remote_copy(
            src_ref=src, dst_ref=dst, send_sem=send, recv_sem=recv,
            device_id=peer, device_id_type=MESH,
        )

    rows = lax.broadcasted_iota(jnp.int32, (T, T), 0)
    cols = lax.broadcasted_iota(jnp.int32, (T, T), 1)
    causal = rows >= cols

    upper = jnp.where(rows <= cols, 1.0, 0.0).astype(F32)
    run[...] = lax.dot_general(
        gate_ref[...], upper, (((1,), (0,)), ((), ())),
        precision=lax.Precision.HIGHEST, preferred_element_type=F32,
    )
    closing_rows = jnp.broadcast_to(run[:, T - 1 : T], (H, W))
    cl[x] = closing_rows.astype(BF16).astype(F32)
    pl.semaphore_wait(barrier, len(peers))

    def c_copy(i):
        return remote(cl.at[x], cl.at[x], c_send.at[i - 1], c_recv.at[i - 1], x_peer(i))

    def x_copy(i, g):
        return remote(
            xg.at[x, g], xg.at[x, g], x_send.at[i - 1, g], x_recv.at[i - 1, g], x_peer(i)
        )

    for i in range(1, X):
        c_copy(i).start()

    def columns(h):
        return pl.ds(pl.multiple_of(h * W, W), W)

    def tables(h):
        by_col = jnp.broadcast_to(run[pl.ds(h, 1), :], (T, T))
        by_row = by_col.T
        closing = by_row[T - 1 : T, :]
        return by_col, by_row, closing

    def local_states(g, carry):
        for hh in range(HP):
            h = g * HP + hh
            _, by_row, closing = tables(h)
            feat_q = nn(q_ref[:, columns(h)], wq_ref[h]).astype(BF16)
            feat_k = (nn(k_ref[:, columns(h)], wk_ref[h]) * key_scale).astype(BF16)
            fq[h] = feat_q
            fk[h] = feat_k
            end_w, start_w = jnp.exp(closing - by_row), jnp.exp(by_row)
            key_w = (feat_k.astype(F32) * end_w).astype(BF16)
            query_w = (feat_q.astype(F32) * start_w).astype(BF16)
            xg[x, g, 0, hh] = tn(key_w, v_ref[:, columns(h)]).astype(BF16)
            xg[x, g, 1, hh] = tn(query_w, o_ref[:, columns(h)]).astype(BF16)
        for i in range(1, X):
            x_copy(i, g).start()
        return carry

    lax.fori_loop(0, NG, local_states, 0)

    def within_block(g, carry):
        for hh in range(HP):
            h = g * HP + hh
            by_col, by_row, _ = tables(h)
            within = jnp.where(causal, jnp.exp(jnp.where(causal, by_row - by_col, 0.0)), 0.0)
            out, val = o_ref[:, columns(h)], v_ref[:, columns(h)]
            feat_q, feat_k = fq[h], fk[h]
            scores = (nt(feat_q, feat_k) * within).astype(BF16)
            grad_scores = (nt(out, val) * within).astype(BF16)
            qt[h] = nn(grad_scores, feat_k)
            kt[h] = tn(grad_scores, feat_q)
            vt[h] = tn(scores, out)
        return carry

    lax.fori_loop(0, NG, within_block, 0)
    for i in range(1, X):
        c_copy(i).wait_recv()

    def along(way, p):
        return p + way * (X - 1 - 2 * p)

    def decay(at, h):
        return jnp.exp(cl[at, pl.ds(h, 1), :])

    def z_copy(way, g):
        return remote(
            zout.at[way, g], zin.at[way, g], z_send.at[way, g], z_recv.at[way, g],
            (dp, (z + 1 - 2 * way) * X + x),
        )

    def ends(way):
        spot = z + way * (Z - 1 - 2 * z)
        return spot > 0, spot < Z - 1

    def chain(way, g):
        has_before, has_after = ends(way)

        @pl.when(has_before)
        def _():
            z_copy(way, g).wait_recv()

        @pl.when(jnp.logical_not(has_before))
        def _():
            zin[way, g] = jnp.zeros(zin.shape[2:], BF16)

        @pl.when(has_after)
        def _():
            for hh in range(HP):
                total = zin[way, g, hh].astype(F32)
                for p in range(X):
                    at = along(way, p)
                    total = total * decay(at, g * HP + hh) + xg[at, g, way, hh].astype(F32)
                zout[way, g, hh] = total.astype(BF16)
            z_copy(way, g).start()

    early_way = jnp.where(z < Z // 2, 0, 1)

    def early(g):
        for i in range(1, X):
            x_copy(i, g).wait_recv()
        chain(early_way, g)

    def carried(way, g, hh):
        spot = x + way * (X - 1 - 2 * x)
        total = zin[way, g, hh].astype(F32)
        for p in range(X - 1):
            at = along(way, p)
            joined = total * decay(at, g * HP + hh) + xg[at, g, way, hh].astype(F32)
            total = jnp.where(p < spot, joined, total)
        return total.astype(BF16)

    def finish(g):
        chain(1 - early_way, g)
        for hh in range(HP):
            h = g * HP + hh
            _, by_row, closing = tables(h)
            end_w, start_w = jnp.exp(closing - by_row), jnp.exp(by_row)
            state_in, grad_in = carried(0, g, hh), carried(1, g, hh)
            que, key = q_ref[:, columns(h)], k_ref[:, columns(h)]
            out, val = o_ref[:, columns(h)], v_ref[:, columns(h)]
            query_back = (qt[h] + nt(out, state_in) * start_w).astype(BF16)
            key_back = ((kt[h] + nt(val, grad_in) * end_w) * key_scale).astype(BF16)
            dv_ref[:, columns(h)] = (vt[h] + nn(fk[h], grad_in) * end_w).astype(BF16)
            dq_ref[:, columns(h)] = nt(query_back, wq_ref[h]).astype(BF16)
            dk_ref[:, columns(h)] = nt(key_back, wk_ref[h]).astype(BF16)
            pm[columns(h), :] = (tn(que, query_back) * map_scale).astype(BF16)
            pm[columns(H + h), :] = (tn(key, key_back) * map_scale).astype(BF16)

    early(0)

    def step(g, carry):
        early(g)
        finish(g - 1)
        return carry

    lax.fori_loop(1, NG, step, 0)
    finish(NG - 1)

    per_y = a2.shape[0]
    per_z, own = a3.shape[0], dm_ref.shape[0]

    def part(yy, cc):
        return pl.ds(pl.multiple_of((yy * 2 + cc) * per_y, per_y), per_y)

    core_copies = [
        remote(pm.at[part(yy, 1 - core)], rc.at[yy], rc_send.at[yy], rc_recv.at[yy], core_peer)
        for yy in range(Y)
    ]
    y_copies = [
        remote(sy.at[i - 1], ry.at[i - 1], ry_send.at[i - 1], ry_recv.at[i - 1], y_peer(i))
        for i in range(1, Y)
    ]
    z_copies = [
        remote(sz.at[i - 1], rz.at[i - 1], rz_send.at[i - 1], rz_recv.at[i - 1], z_peer(i))
        for i in range(1, Z)
    ]
    x_copies = [
        remote(sx.at[i - 1], rx.at[i - 1], rx_send.at[i - 1], rx_recv.at[i - 1], x_peer(i))
        for i in range(1, X)
    ]
    for copy in core_copies:
        copy.start()
    for copy in core_copies:
        copy.wait_recv()
    for i in range(1, Y):
        yt = lax.rem(y + i, Y)
        sy[i - 1] = (pm[part(yt, core), :].astype(F32) + rc[yt].astype(F32)).astype(BF16)
        y_copies[i - 1].start()
    a2[...] = pm[part(y, core), :].astype(F32) + rc[y].astype(F32)
    for i in range(1, Y):
        y_copies[i - 1].wait_recv()
        a2[...] += ry[i - 1].astype(F32)
    for i in range(1, Z):
        zt = lax.rem(z + i, Z)
        sz[i - 1] = a2[pl.ds(pl.multiple_of(zt * per_z, per_z), per_z), :].astype(BF16)
        z_copies[i - 1].start()
    a3[...] = a2[pl.ds(pl.multiple_of(z * per_z, per_z), per_z), :]
    for i in range(1, Z):
        z_copies[i - 1].wait_recv()
        a3[...] += rz[i - 1].astype(F32)
    for i in range(1, X):
        xt = lax.rem(x + i, X)
        sx[i - 1] = a3[pl.ds(pl.multiple_of(xt * own, own), own), :].astype(sx.dtype)
        x_copies[i - 1].start()
    total = a3[pl.ds(pl.multiple_of(x * own, own), own), :]
    for i in range(1, X):
        x_copies[i - 1].wait_recv()
        total = total + rx[i - 1].astype(F32)
    dm_ref[...] = total

    for copy in core_copies + y_copies + z_copies + x_copies:
        copy.wait_send()
    for i in range(1, X):
        c_copy(i).wait_send()
    for way in range(2):
        @pl.when(ends(way)[1])
        def _():
            for g in range(NG):
                z_copy(way, g).wait_send()
    for g in range(NG):
        for i in range(1, X):
            x_copy(i, g).wait_send()


def solution(mesh):
    n_dp, n_ctx = mesh.shape["dp"], mesh.shape["context"]
    X = 1
    while 2 * (2 * X) ** 2 <= n_ctx:
        X *= 2
    Z, Y = n_ctx // X, n_dp // 2

    def per_device(queries, keys, values, out_grad, log_gates, query_map, key_map):
        H, W = query_map.shape[:2]
        T = queries.shape[1]
        NG = 4
        HP = H // NG
        own = 2 * H * W // (n_dp * n_ctx)
        map_scale = float(T * n_ctx * n_dp * queries.shape[0]) ** (-0.5)
        sizes = (Y, Z, X, H, W, T, NG, HP, map_scale)
        per_y, per_z = own * X * Z, own * X
        last = BF16 if own % 16 == 0 else F32
        dma = pltpu.SemaphoreType.DMA
        vmem = pl.BlockSpec(memory_space=pltpu.VMEM)
        grads = pl.pallas_call(
            functools.partial(kernel, sizes),
            out_shape=[jax.ShapeDtypeStruct((T, H * W), BF16)] * 3
            + [jax.ShapeDtypeStruct((own, W), F32)],
            in_specs=[vmem] * 7,
            out_specs=[vmem] * 4,
            scratch_shapes=[
                pltpu.VMEM((H, T), F32),
                pltpu.VMEM((H, T, W), BF16),
                pltpu.VMEM((H, T, W), BF16),
                pltpu.VMEM((H, T, W), F32),
                pltpu.VMEM((H, T, W), F32),
                pltpu.VMEM((H, T, W), F32),
                pltpu.VMEM((X, NG, 2, HP, W, W), BF16),
                pltpu.VMEM((X, H, W), F32),
                pltpu.VMEM((2, NG, HP, W, W), BF16),
                pltpu.VMEM((2, NG, HP, W, W), BF16),
                pltpu.VMEM((2 * H * W, W), BF16),
                pltpu.VMEM((Y, per_y, W), BF16),
                pltpu.VMEM((Y - 1, per_y, W), BF16),
                pltpu.VMEM((Y - 1, per_y, W), BF16),
                pltpu.VMEM((per_y, W), F32),
                pltpu.VMEM((Z - 1, per_z, W), BF16),
                pltpu.VMEM((Z - 1, per_z, W), BF16),
                pltpu.VMEM((per_z, W), F32),
                pltpu.VMEM((X - 1, own, W), last),
                pltpu.VMEM((X - 1, own, W), last),
                dma((X - 1,)), dma((X - 1,)),
                dma((X - 1, NG)), dma((X - 1, NG)),
                dma((2, NG)), dma((2, NG)),
                dma((Y,)), dma((Y,)),
                dma((Y - 1,)), dma((Y - 1,)),
                dma((Z - 1,)), dma((Z - 1,)),
                dma((X - 1,)), dma((X - 1,)),
            ],
            compiler_params=pltpu.CompilerParams(
                collective_id=0, has_side_effects=True, vmem_limit_bytes=48 * 1024 * 1024
            ),
        )(queries[0], keys[0], values[0], out_grad[0], log_gates[0], query_map, key_map)
        return grads[0][None], grads[1][None], grads[2][None], grads[3]

    return jax.shard_map(
        per_device,
        mesh=mesh,
        in_specs=(
            P("dp", "context", None),
            P("dp", "context", None),
            P("dp", "context", None),
            P("dp", "context", None),
            P("dp", None, "context"),
            P(),
            P(),
        ),
        out_specs=(
            P("dp", "context", None),
            P("dp", "context", None),
            P("dp", "context", None),
            P(("dp", "context"), None),
        ),
        check_vma=False,
    )
```
